32 devices in a mesh: groups: 2 (over x), depth: 16 (over z, y, core).
Axes of the slice: x: 2, y: 2, z: 4, core: 2. Of those that a mesh axis runs over, the one named last changes fastest.
Arguments:
- fronts: bfloat16 [4, 64, 8, 2048], P(None, ('groups', 'depth')), parts along dimension 1, may hold values from -6 to 6
- extrap: bfloat16 [32, 16, 5, 2, 128, 128], P('depth'), may hold values from -0.15625 to 0.15625
- offsets: int32 [2, 5], replicated, may hold values from -2 to 2
- assign: int32 [2, 8], replicated, may hold values from 0 to 7, each once within a row
Outputs:
- images: float32 [8, 32, 2048], P(None, ('groups', 'depth')), parts along dimension 1
- last_fronts: bfloat16 [4, 64, 8, 2048], P(None, ('groups', 'depth')), parts along dimension 1
The draws below stay inside these ranges and needn't reach their ends.
There are 2 independent parts, one for each index of `groups`. The reference program is written for one: setup_inputs(seed, part) draws one part's arguments, and reference() takes and returns one part's arrays. A program takes and returns all parts, laid end to end along the dimension named above; an argument that names none is the same for every part. Nothing has to cross between parts.
Inputs may be any that keep to these rules, and one draw needn't show every extreme that they name: `assign`: each row names every shot number once.
All inputs are finite; a program needn't handle non-finite values.
Results may differ from the reference program's by a relative error of at most 0.015.
Values may be sent and summed in bfloat16 or wider, within the bound.
No kernel may reach another device: no remote copies, remote signals or barrier semaphores. Data moves between devices by JAX's collectives and lax.ppermute only.
A program may use at most 64 MiB of HBM per device.

```python
import math
import jax
import jax.numpy as jnp
from jax import lax

BLOCK = 128
NBLK = 16
BAND = 5
HANDOVERS = 8
SHOTS = 8
X = 2048
NFREQ = 16
SECTIONS = 2


def plant(result, own_key, smallest, top_value):
    longest = result.shape.index(max(result.shape))
    spots = []
    for shift in (0, 1):
        where = [jax.random.randint(jax.random.fold_in(own_key, axis), (), 0, length) for axis, length in enumerate(result.shape)]
        where[longest] = (where[longest] + shift) % result.shape[longest]
        spots.append(tuple(where))
    return result.at[spots[0]].set(smallest).at[spots[1]].set(top_value)


def block_scale(own_key, extent, split, least, high):
    gain, own = 1.0, jax.random.fold_in(own_key, 6)
    for position, parts in split:
        draws = jnp.exp(jax.random.uniform(jax.random.fold_in(own, position), (parts,), jnp.float32, least / len(split), high / len(split)))
        gain = gain * jnp.repeat(draws, extent[position] // parts).reshape([-1 if axis == position else 1 for axis in range(len(extent))])
    return gain


def noise(own_key, shape, spread, limit, cuts=(), kind=jnp.bfloat16):
    drawn = spread * jax.random.normal(own_key, shape, jnp.float32)
    if cuts:
        drawn = drawn * block_scale(own_key, shape, cuts, -0.22, 0.18)
    return jnp.clip(drawn, -limit, limit).astype(kind)


def setup_inputs(seed: int = 0, part: int = 0) -> dict:
    keys = jax.random.split(jax.random.key(seed), 5)
    part_keys = jax.random.split(jax.random.fold_in(keys[4], part), 5)
    return {
        "fronts": noise(part_keys[0], (4, SECTIONS * NFREQ, SHOTS, X), 1.0, 6.0, ((1, 16),)),
        "extrap": noise(keys[1], (SECTIONS * NFREQ, NBLK, BAND, 2, BLOCK, BLOCK), (2 * BAND * BLOCK) ** -0.5, 0.15625, ((0, 16),)),
        "offsets": plant(jax.random.randint(keys[2], (SECTIONS, BAND), -(BAND // 2), BAND // 2 + 1), jax.random.fold_in(keys[2], 1), -(BAND // 2), (BAND // 2 + 1) - 1).astype(jnp.int32),
        "assign": jax.vmap(lambda own: jax.random.permutation(own, SHOTS))(jax.random.split(keys[3], SECTIONS)).reshape((SECTIONS, SHOTS)).astype(jnp.int32),
    }


def advance(wave_state, band_offsets, operator):
    reach = BAND // 2
    blocks = wave_state.reshape(4, NFREQ, SHOTS, NBLK, BLOCK)
    padded = jnp.pad(blocks, ((0, 0), (0, 0), (0, 0), (reach, reach), (0, 0)))
    shifted = jnp.stack([lax.dynamic_slice_in_dim(padded, band_offsets[band_pos] + reach, NBLK, 3) for band_pos in range(BAND)], axis=3)
    products = jnp.einsum('cfskbj,fbkpjl->pcfsbl', shifted.astype(jnp.float32), operator.astype(jnp.float32), precision=lax.Precision.HIGHEST)
    real_prod = products[0]
    imag_prod = products[1]
    src_real = real_prod[0] - imag_prod[1]
    src_imag = imag_prod[0] + real_prod[1]
    rec_real = real_prod[2] + imag_prod[3]
    rec_imag = real_prod[3] - imag_prod[2]
    joined = jnp.stack([src_real, src_imag, rec_real, rec_imag])
    return joined.reshape(4, NFREQ, SHOTS, X).astype(jnp.bfloat16)

def reference(fronts, extrap, offsets, assign):
    operators = extrap.reshape(SECTIONS, NFREQ, NBLK, BAND, 2, BLOCK, BLOCK)
    wave_state = jnp.moveaxis(fronts.reshape(4, SECTIONS, NFREQ, SHOTS, X), 1, 0)
    image_scale = 1.0 / math.sqrt(2.0 * NFREQ)
    section_rows = jnp.arange(SECTIONS, dtype=jnp.int32)[:, None]
    images = []
    for handover in range(HANDOVERS):
        wave_state = lax.map(lambda section_item: advance(section_item[0], section_item[1], section_item[2]), (wave_state, offsets, operators))
        fields = wave_state.astype(jnp.float32)
        partial_value = image_scale * lax.optimization_barrier(jnp.sum(fields[:, 0] * fields[:, 2] + fields[:, 1] * fields[:, 3], axis=1))
        placed = jnp.zeros_like(partial_value).at[section_rows, assign].set(partial_value)
        images.append(placed.reshape(SECTIONS * SHOTS, X))
        if handover + 1 < HANDOVERS:
            wave_state = jnp.concatenate([wave_state[-1:], wave_state[:-1]], axis=0)
    last_fronts = jnp.moveaxis(wave_state, 0, 1).reshape(4, SECTIONS * NFREQ, SHOTS, X)
    return (jnp.stack(images), last_fronts)
```

```python
import functools
import math

import jax
import jax.numpy as jnp
from jax import lax
from jax.experimental import pallas as pl
from jax.experimental.pallas import tpu as pltpu
from jax.sharding import PartitionSpec as P

BLOCK = 128
HANDOVERS = 8


def advance_blocks(offs, rows, e_ref, pad_ref, adv_ref, img_ref, scale, blocks, band, slots):
    for b in blocks:
        lhs = jnp.concatenate([pad_ref[b + offs[k]] for k in range(band)], axis=1)
        er = e_ref[b, :, 0].reshape(band * BLOCK, BLOCK)
        ei = e_ref[b, :, 1].reshape(band * BLOCK, BLOCK)
        p = jnp.dot(lhs, er, preferred_element_type=jnp.float32)
        q = jnp.dot(lhs, ei, preferred_element_type=jnp.float32)
        p = [p[c * slots : (c + 1) * slots] for c in range(4)]
        q = [q[c * slots : (c + 1) * slots] for c in range(4)]
        new = jnp.concatenate([p[0] - q[1], q[0] + p[1], p[2] + q[3], p[3] - q[2]], axis=0)
        new = new.astype(jnp.bfloat16)
        adv_ref[b] = new
        f = new.astype(jnp.float32)
        f = [f[c * slots : (c + 1) * slots] for c in range(4)]
        part = scale * (f[0] * f[2] + f[1] * f[3])
        for j in range(slots):
            at = (pl.ds(rows[j], 1), b)
            img_ref[at] = part[j : j + 1]


def zero_edges(pad_ref, reach):
    nblk = pad_ref.shape[0] - 2 * reach
    edge = jnp.zeros((reach,) + pad_ref.shape[1:], pad_ref.dtype)
    pad_ref[:reach] = edge
    pad_ref[reach + nblk :] = edge


def first_kernel(scale, sec_ref, offs_hbm, asgs_hbm, e_hbm, w_hbm, *rest):
    adv_ref, img_ref, code_ref = rest[:3]
    freqs = w_hbm.shape[1]
    later = rest[3 : 3 + freqs - 1]
    e_ref, pad_ref, off_ref, asg_ref, w_ref, e_sems, w_sems = rest[3 + freqs - 1 :]
    nblk, band = e_ref.shape[:2]
    slots = w_ref.shape[2]
    reach = band // 2
    loads = [
        pltpu.make_async_copy(w_hbm, w_ref, w_sems.at[0]),
        pltpu.make_async_copy(offs_hbm, off_ref, w_sems.at[1]),
        pltpu.make_async_copy(asgs_hbm, asg_ref, w_sems.at[2]),
    ]
    for c in loads:
        c.start()
    copies = stream(e_hbm, e_ref, e_sems, 0)
    zero_edges(pad_ref, reach)
    for c in loads:
        c.wait()
    for f in range(freqs):
        for b in range(nblk):
            cols = slice(b * BLOCK, (b + 1) * BLOCK)
            block = [w_ref[c, f, :, cols].astype(jnp.float32) for c in range(4)]
            block = jnp.concatenate(block, axis=0).astype(jnp.bfloat16)
            if f == 0:
                pad_ref[reach + b] = block
            else:
                later[f - 1][b] = block
    sec = sec_ref[0]
    offs = [off_ref[sec, k] + reach for k in range(band)]
    rows = [asg_ref[sec, j] for j in range(slots)]
    for k, value in enumerate(offs + rows):
        code_ref[k] = jnp.full(code_ref.shape[1:], value, jnp.int32)
    for c, blocks in copies:
        c.wait()
        advance_blocks(
            offs, rows, e_ref, pad_ref, adv_ref, img_ref, scale, blocks, band, slots
        )


def stream(e_hbm, e_ref, sems, f):
    parts = sems.shape[0]
    per = e_ref.shape[0] // parts
    copies = []
    for i in range(parts):
        at = pl.ds(i * per, per)
        copies.append(pltpu.make_async_copy(e_hbm.at[f, at], e_ref.at[at], sems.at[i]))
        copies[-1].start()
    return [(c, range(i * per, (i + 1) * per)) for i, c in enumerate(copies)]


def next_kernel(scale, f, code_ref, e_hbm, w_ref, tok, adv_ref, img_ref, e_ref, pad_ref, e_sems):
    copies = stream(e_hbm, e_ref, e_sems, f)
    nblk, band = e_ref.shape[:2]
    reach = band // 2
    slots = img_ref.shape[0]
    code = [code_ref[k][0, 0] for k in range(band + slots)]
    zero_edges(pad_ref, reach)
    pad_ref[reach : reach + nblk] = w_ref[...]
    for c, blocks in copies:
        c.wait()
        advance_blocks(
            code[:band], code[band:], e_ref, pad_ref, adv_ref, img_ref, scale, blocks, band, slots
        )


def step_kernel(scale, f, code_ref, e_ref, w_ref, adv_ref, img_ref, pad_ref):
    nblk, band = e_ref.shape[1:3]
    reach = band // 2
    slots = img_ref.shape[0]
    code = [code_ref[k][0, 0] for k in range(band + slots)]
    zero_edges(pad_ref, reach)
    pad_ref[reach : reach + nblk] = w_ref[...]
    advance_blocks(
        code[:band], code[band:], e_ref.at[f], pad_ref, adv_ref, img_ref, scale, range(nblk),
        band, slots,
    )


SMEM = pl.BlockSpec(memory_space=pltpu.SMEM)
VMEM = pl.BlockSpec(memory_space=pltpu.VMEM)
HBM = pl.BlockSpec(memory_space=pltpu.HBM)
ANY = pl.BlockSpec(memory_space=pl.ANY)


def held(x, space):
    return pltpu.with_memory_space_constraint(x, space)


def cost(e_shape, rows):
    macs = math.prod(e_shape) * rows
    return pl.CostEstimate(flops=2 * macs, bytes_accessed=BLOCK, transcendentals=0)


def run_first(sec, offsets, assign, extrap, fronts, scale):
    nblk, band = extrap.shape[1:3]
    nfield, freqs, slots, points = fronts.shape
    rows = nfield * slots
    parts = math.gcd(4, nblk)
    wave = pltpu.VMEM((nblk, rows, BLOCK), jnp.bfloat16)
    return pl.pallas_call(
        functools.partial(first_kernel, scale),
        out_shape=(
            wave,
            pltpu.VMEM((slots, nblk, BLOCK), jnp.float32),
            pltpu.VMEM((band + slots, 8, BLOCK), jnp.int32),
        )
        + (wave,) * (freqs - 1),
        in_specs=[SMEM, HBM, HBM, HBM, HBM],
        out_specs=(VMEM,) * (2 + freqs),
        scratch_shapes=[
            pltpu.VMEM(extrap.shape[1:], extrap.dtype),
            pltpu.VMEM((nblk + 2 * (band // 2), rows, BLOCK), jnp.bfloat16),
            pltpu.SMEM(offsets.shape, jnp.int32),
            pltpu.SMEM(assign.shape, jnp.int32),
            pltpu.VMEM(fronts.shape, fronts.dtype),
            pltpu.SemaphoreType.DMA((parts,)),
            pltpu.SemaphoreType.DMA((3,)),
        ],
        compiler_params=pltpu.CompilerParams(vmem_limit_bytes=8 * 2**20),
        cost_estimate=cost(extrap.shape[1:], rows),
        name="first",
    )(held(sec, pltpu.SMEM), *[held(x, pltpu.HBM) for x in (offsets, assign, extrap, fronts)])


def run_step(f, code, e, w, scale, token=None):
    streamed = token is not None
    nblk, band = e.shape[1:3]
    rows = w.shape[1]
    pad = pltpu.VMEM((nblk + 2 * (band // 2), rows, BLOCK), jnp.bfloat16)
    scratch = [pad]
    if streamed:
        parts = math.gcd(4, nblk)
        scratch = [pltpu.VMEM(e.shape[1:], e.dtype), pad, pltpu.SemaphoreType.DMA((parts,))]
    return pl.pallas_call(
        functools.partial(next_kernel if streamed else step_kernel, scale, f),
        out_shape=(
            pltpu.VMEM((nblk, rows, BLOCK), jnp.bfloat16),
            pltpu.VMEM((rows // 4, nblk, BLOCK), jnp.float32),
        ),
        in_specs=[VMEM, HBM if streamed else VMEM, VMEM] + ([ANY] if streamed else []),
        out_specs=(VMEM, VMEM),
        scratch_shapes=scratch,
        compiler_params=pltpu.CompilerParams(vmem_limit_bytes=(8 if streamed else 4) * 2**20),
        cost_estimate=cost(e.shape[1:], rows),
        name="next" if streamed else "step",
    )(
        held(code, pltpu.VMEM),
        held(e, pltpu.HBM if streamed else pltpu.VMEM),
        held(w, pltpu.VMEM),
        *([token] if streamed else []),
    )


def fold_owners(partial, me, owners):
    bit = owners // 2
    size = lax.axis_size("depth")
    while bit:
        half = partial.shape[0] // 2
        lower, upper = partial[:half], partial[half:]
        mine_up = me // bit % 2 == 1
        outgoing = jnp.where(mine_up, lower, upper)
        kept = jnp.where(mine_up, upper, lower)
        partial = kept + lax.ppermute(outgoing, "depth", [(i, i ^ bit) for i in range(size)])
        bit //= 2
    return partial


def on_device(fronts, extrap, offsets, assign):
    sections = offsets.shape[0]
    size = lax.axis_size("depth")
    owners = size // sections
    index = lax.axis_index("depth")
    section, me = index // owners, index % owners
    sec = section.astype(jnp.int32)[None]
    nfield, freqs, slots, points = fronts.shape
    nblk = extrap.shape[1]
    scale = 1.0 / math.sqrt(2.0 * owners * freqs)
    onward = [(i, (i + owners) % size) for i in range(size)]
    waves, images = [None] * freqs, []
    for r in range(HANDOVERS):
        parts = []
        for f in range(freqs):
            if r == 0 and f == 0:
                adv, img, code, *later = run_first(sec, offsets, assign, extrap, fronts, scale)
                token = lax.ppermute(img[:1], "depth", [(i, i ^ 1) for i in range(size)])
            elif r == 0:
                adv, img = run_step(f, code, extrap, later[f - 1], scale, token)
            else:
                adv, img = run_step(f, code, extrap, waves[f], scale)
            parts.append(img)
            waves[f] = lax.ppermute(adv, "depth", onward) if r + 1 < HANDOVERS else adv
        images.append(sum(parts[1:], parts[0]))
    early = fold_owners(jnp.stack(images[:-1], axis=1), me, owners)
    late = fold_owners(jnp.stack(images[-1:], axis=1), me, owners)
    images = jnp.concatenate([early, late], axis=1).reshape(HANDOVERS, 1, points)
    last = jnp.stack(waves).reshape(freqs, nblk, nfield, slots, BLOCK)
    last = last.transpose(2, 0, 3, 1, 4).reshape(fronts.shape)
    return images, last


def solution(mesh):
    placed = (
        P(None, ("groups", "depth"), None, None),
        P("depth", None, None, None, None, None),
        P(),
        P(),
    )
    return jax.shard_map(
        on_device,
        mesh=mesh,
        in_specs=placed,
        out_specs=(P(None, ("groups", "depth"), None), P(None, ("groups", "depth"), None, None)),
        check_vma=False,
    )
```

```python
import functools
import math

import jax
import jax.numpy as jnp
from jax import lax
from jax.experimental import pallas as pl
from jax.experimental.pallas import tpu as pltpu
from jax.sharding import PartitionSpec as P

BLOCK = 128
HANDOVERS = 8
PARTS = 4


def advance_blocks(offs, rows, e_ref, pad_ref, adv_ref, img_ref, scale, blocks, band, slots):
    for b in blocks:
        lhs = jnp.concatenate([pad_ref[b + offs[k]] for k in range(band)], axis=1)
        er = e_ref[b, :, 0].reshape(band * BLOCK, BLOCK)
        ei = e_ref[b, :, 1].reshape(band * BLOCK, BLOCK)
        p = jnp.dot(lhs, er, preferred_element_type=jnp.float32)
        q = jnp.dot(lhs, ei, preferred_element_type=jnp.float32)
        p = [p[c * slots : (c + 1) * slots] for c in range(4)]
        q = [q[c * slots : (c + 1) * slots] for c in range(4)]
        new = jnp.concatenate([p[0] - q[1], q[0] + p[1], p[2] + q[3], p[3] - q[2]], axis=0)
        new = new.astype(jnp.bfloat16)
        adv_ref[b] = new
        f = new.astype(jnp.float32)
        f = [f[c * slots : (c + 1) * slots] for c in range(4)]
        part = scale * (f[0] * f[2] + f[1] * f[3])
        for j in range(slots):
            at = (pl.ds(rows[j], 1), b)
            img_ref[at] = part[j : j + 1]


def zero_edges(pad_ref, reach):
    nblk = pad_ref.shape[0] - 2 * reach
    edge = jnp.zeros((reach,) + pad_ref.shape[1:], pad_ref.dtype)
    pad_ref[:reach] = edge
    pad_ref[reach + nblk :] = edge


def stream(e_hbm, e_ref, sems):
    parts = sems.shape[0]
    per = e_ref.shape[0] // parts
    copies = []
    for i in range(parts):
        at = pl.ds(i * per, per)
        copies.append(pltpu.make_async_copy(e_hbm.at[at], e_ref.at[at], sems.at[i]))
        copies[-1].start()
    return [(c, range(i * per, (i + 1) * per)) for i, c in enumerate(copies)]


def fill_blocks(w_ref, pad_ref, reach):
    for b in range(pad_ref.shape[0] - 2 * reach):
        cols = slice(b * BLOCK, (b + 1) * BLOCK)
        block = [w_ref[c, :, cols].astype(jnp.float32) for c in range(4)]
        pad_ref[reach + b] = jnp.concatenate(block, axis=0).astype(jnp.bfloat16)


def read_code(code_ref, band, slots):
    code = [code_ref[k][0, 0] for k in range(band + slots)]
    return code[:band], code[band:]


def first_kernel(
    scale, place_ref, offs_hbm, asgs_hbm, e_hbm, w_hbm, adv_ref, img_ref, code_ref, e_all,
    pad_ref, off_ref, asg_ref, w_ref, e_sems, w_sems,
):
    e_ref = e_all.at[0]
    nblk, band = e_ref.shape[:2]
    slots = w_ref.shape[1]
    reach = band // 2
    loads = [
        pltpu.make_async_copy(w_hbm.at[:, 0], w_ref, w_sems.at[0]),
        pltpu.make_async_copy(offs_hbm, off_ref, w_sems.at[1]),
        pltpu.make_async_copy(asgs_hbm, asg_ref, w_sems.at[2]),
    ]
    for c in loads:
        c.start()
    copies = stream(e_hbm.at[0], e_ref, e_sems)
    zero_edges(pad_ref, reach)
    for c in loads:
        c.wait()
    fill_blocks(w_ref, pad_ref, reach)
    sec, me = place_ref[0], place_ref[1]
    offs = [off_ref[sec, k] + reach for k in range(band)]
    rows = [asg_ref[sec, j] for j in range(slots)]
    for k, value in enumerate(offs + rows + [me]):
        code_ref[k] = jnp.full(code_ref.shape[1:], value, jnp.int32)
    for c, blocks in copies:
        c.wait()
        advance_blocks(
            offs, rows, e_ref, pad_ref, adv_ref, img_ref, scale, blocks, band, slots
        )


def next_kernel(
    scale, f, code_ref, old, e_hbm, w_hbm, tok, adv_ref, img_ref, e_all,
    pad_ref, w_ref, e_sems, w_sem,
):
    e_ref = e_all.at[f]
    load = pltpu.make_async_copy(w_hbm.at[:, f], w_ref, w_sem.at[0])
    load.start()
    copies = stream(e_hbm.at[f], e_ref, e_sems)
    nblk, band = e_ref.shape[:2]
    reach = band // 2
    slots = img_ref.shape[0]
    offs, rows = read_code(code_ref, band, slots)
    zero_edges(pad_ref, reach)
    load.wait()
    fill_blocks(w_ref, pad_ref, reach)
    for c, blocks in copies:
        c.wait()
        advance_blocks(
            offs, rows, e_ref, pad_ref, adv_ref, img_ref, scale, blocks, band, slots
        )


def step_kernel(scale, f, code_ref, e_ref, w_ref, adv_ref, img_ref, pad_ref):
    nblk, band = e_ref.shape[1:3]
    reach = band // 2
    slots = img_ref.shape[0]
    offs, rows = read_code(code_ref, band, slots)
    zero_edges(pad_ref, reach)
    pad_ref[reach : reach + nblk] = w_ref[...]
    advance_blocks(
        offs, rows, e_ref.at[f], pad_ref, adv_ref, img_ref, scale, range(nblk), band, slots
    )


def split_kernel(bit, freqs, code_ref, *refs):
    ins, (keep_ref, send_ref) = refs[:-2], refs[-2:]
    side = (code_ref[code_ref.shape[0] - 1][0, 0] >> bit) & 1
    halves, rounds = keep_ref.shape[:2]
    for half in range(halves):
        for out, row in ((keep_ref, 2 * half + side), (send_ref, 2 * half + 1 - side)):
            for r in range(rounds):
                if bit == 0:
                    value = ins[r * freqs][row]
                    for f in range(1, freqs):
                        value += ins[r * freqs + f][row]
                else:
                    value = ins[0][row, r] + ins[1][row, r].astype(jnp.float32)
                out[half, r] = value.astype(out.dtype)


SMEM = pl.BlockSpec(memory_space=pltpu.SMEM)
VMEM = pl.BlockSpec(memory_space=pltpu.VMEM)
HBM = pl.BlockSpec(memory_space=pltpu.HBM)
ANY = pl.BlockSpec(memory_space=pl.ANY)


def held(x, space):
    return pltpu.with_memory_space_constraint(x, space)


def cost(e_shape, rows):
    macs = math.prod(e_shape) * rows
    return pl.CostEstimate(flops=2 * macs, bytes_accessed=BLOCK, transcendentals=0)


def run_first(place, offsets, assign, extrap, fronts, scale):
    nblk, band = extrap.shape[1:3]
    nfield, freqs, slots, points = fronts.shape
    rows = nfield * slots
    parts = math.gcd(PARTS, nblk)
    return pl.pallas_call(
        functools.partial(first_kernel, scale),
        out_shape=(
            pltpu.VMEM((nblk, rows, BLOCK), jnp.bfloat16),
            pltpu.VMEM((slots, nblk, BLOCK), jnp.float32),
            pltpu.VMEM((band + slots + 1, 8, BLOCK), jnp.int32),
            pltpu.VMEM(extrap.shape, extrap.dtype),
        ),
        in_specs=[SMEM, HBM, HBM, HBM, HBM],
        out_specs=(VMEM,) * 4,
        scratch_shapes=[
            pltpu.VMEM((nblk + 2 * (band // 2), rows, BLOCK), jnp.bfloat16),
            pltpu.SMEM(offsets.shape, jnp.int32),
            pltpu.SMEM(assign.shape, jnp.int32),
            pltpu.VMEM((nfield, slots, points), fronts.dtype),
            pltpu.SemaphoreType.DMA((parts,)),
            pltpu.SemaphoreType.DMA((3,)),
        ],
        compiler_params=pltpu.CompilerParams(vmem_limit_bytes=4 * 2**20),
        cost_estimate=cost(extrap.shape[1:], rows),
        name="first",
    )(held(place, pltpu.SMEM), *[held(x, pltpu.HBM) for x in (offsets, assign, extrap, fronts)])


def run_next(f, code, e, extrap, fronts, token, scale):
    nblk, band = e.shape[1:3]
    nfield, freqs, slots, points = fronts.shape
    rows = nfield * slots
    parts = math.gcd(PARTS, nblk)
    return pl.pallas_call(
        functools.partial(next_kernel, scale, f),
        out_shape=(
            pltpu.VMEM((nblk, rows, BLOCK), jnp.bfloat16),
            pltpu.VMEM((slots, nblk, BLOCK), jnp.float32),
            pltpu.VMEM(e.shape, e.dtype),
        ),
        in_specs=[VMEM, VMEM, HBM, HBM, ANY],
        out_specs=(VMEM,) * 3,
        scratch_shapes=[
            pltpu.VMEM((nblk + 2 * (band // 2), rows, BLOCK), jnp.bfloat16),
            pltpu.VMEM((nfield, slots, points), fronts.dtype),
            pltpu.SemaphoreType.DMA((parts,)),
            pltpu.SemaphoreType.DMA((1,)),
        ],
        input_output_aliases={1: 2},
        compiler_params=pltpu.CompilerParams(vmem_limit_bytes=4 * 2**20),
        cost_estimate=cost(e.shape[1:], rows),
        name="next",
    )(held(code, pltpu.VMEM), held(e, pltpu.VMEM), held(extrap, pltpu.HBM), held(fronts, pltpu.HBM), token)


def run_step(f, code, e, w, scale):
    nblk, band = e.shape[1:3]
    rows = w.shape[1]
    return pl.pallas_call(
        functools.partial(step_kernel, scale, f),
        out_shape=(
            pltpu.VMEM((nblk, rows, BLOCK), jnp.bfloat16),
            pltpu.VMEM((rows // 4, nblk, BLOCK), jnp.float32),
        ),
        in_specs=[VMEM, VMEM, VMEM],
        out_specs=(VMEM, VMEM),
        scratch_shapes=[pltpu.VMEM((nblk + 2 * (band // 2), rows, BLOCK), jnp.bfloat16)],
        compiler_params=pltpu.CompilerParams(vmem_limit_bytes=4 * 2**20),
        cost_estimate=cost(e.shape[1:], rows),
        name="step",
    )(*[held(x, pltpu.VMEM) for x in (code, e, w)])


def fold_owners(code, parts, rounds, owners):
    size = lax.axis_size("depth")
    rows, nblk, lanes = parts[0].shape
    freqs = len(parts) // rounds
    ins, bit = parts, 0
    while 1 << bit < owners:
        rows //= 2
        half = (rows, rounds, nblk, lanes)
        keep, send = pl.pallas_call(
            functools.partial(split_kernel, bit, freqs),
            out_shape=(pltpu.VMEM(half, jnp.float32), pltpu.VMEM(half, jnp.bfloat16)),
            in_specs=[VMEM] * (1 + len(ins)),
            out_specs=(VMEM, VMEM),
            compiler_params=pltpu.CompilerParams(vmem_limit_bytes=4 * 2**20),
            cost_estimate=pl.CostEstimate(flops=BLOCK, bytes_accessed=BLOCK, transcendentals=0),
            name="split",
        )(*[held(x, pltpu.VMEM) for x in (code, *ins)])
        came = lax.ppermute(send, "depth", [(i, i ^ (1 << bit)) for i in range(size)])
        ins = (keep, came)
        bit += 1
    return ins[0] + ins[1].astype(jnp.float32)


def on_device(fronts, extrap, offsets, assign):
    sections = offsets.shape[0]
    size = lax.axis_size("depth")
    owners = size // sections
    index = lax.axis_index("depth")
    place = jnp.stack([lax.div(index, owners), lax.rem(index, owners)]).astype(jnp.int32)
    nfield, freqs, slots, points = fronts.shape
    nblk = extrap.shape[1]
    scale = 1.0 / math.sqrt(2.0 * owners * freqs)
    onward = [(i, (i + owners) % size) for i in range(size)]
    waves, parts = [None] * freqs, []
    for r in range(HANDOVERS):
        for f in range(freqs):
            if r == 0 and f == 0:
                adv, img, code, e = run_first(place, offsets, assign, extrap, fronts, scale)
                token = lax.ppermute(img[:1], "depth", [(i, i ^ 1) for i in range(size)])
            elif r == 0:
                adv, img, e = run_next(f, code, e, extrap, fronts, token, scale)
            else:
                adv, img = run_step(f, code, e, waves[f], scale)
            parts.append(img)
            waves[f] = lax.ppermute(adv, "depth", onward) if r + 1 < HANDOVERS else adv
    images = fold_owners(code, parts, HANDOVERS, owners).reshape(HANDOVERS, 1, points)
    last = jnp.stack(waves).reshape(freqs, nblk, nfield, slots, BLOCK)
    last = last.transpose(2, 0, 3, 1, 4).reshape(fronts.shape)
    return images, last


def solution(mesh):
    placed = (
        P(None, ("groups", "depth"), None, None),
        P("depth", None, None, None, None, None),
        P(),
        P(),
    )
    return jax.shard_map(
        on_device,
        mesh=mesh,
        in_specs=placed,
        out_specs=(P(None, ("groups", "depth"), None), P(None, ("groups", "depth"), None, None)),
        check_vma=False,
    )
```

```python
import functools
import math

import jax
import jax.numpy as jnp
from jax import lax
from jax.experimental import pallas as pl
from jax.experimental.pallas import tpu as pltpu
from jax.sharding import PartitionSpec as P

BLOCK = 128
HANDOVERS = 8
PARTS = 4


def advance_blocks(offs, rows, e_ref, pad_ref, adv_ref, img_ref, scale, blocks, band, slots):
    for b in blocks:
        lhs = jnp.concatenate([pad_ref[b + offs[k]] for k in range(band)], axis=1)
        er = e_ref[b, :, 0].reshape(band * BLOCK, BLOCK)
        ei = e_ref[b, :, 1].reshape(band * BLOCK, BLOCK)
        p = jnp.dot(lhs, er, preferred_element_type=jnp.float32)
        q = jnp.dot(lhs, ei, preferred_element_type=jnp.float32)
        p = [p[c * slots : (c + 1) * slots] for c in range(4)]
        q = [q[c * slots : (c + 1) * slots] for c in range(4)]
        new = jnp.concatenate([p[0] - q[1], q[0] + p[1], p[2] + q[3], p[3] - q[2]], axis=0)
        new = new.astype(jnp.bfloat16)
        adv_ref[b] = new
        f = new.astype(jnp.float32)
        f = [f[c * slots : (c + 1) * slots] for c in range(4)]
        part = scale * (f[0] * f[2] + f[1] * f[3])
        for j in range(slots):
            at = (pl.ds(rows[j], 1), b)
            img_ref[at] = part[j : j + 1]


def zero_edges(pad_ref, reach):
    nblk = pad_ref.shape[0] - 2 * reach
    edge = jnp.zeros((reach,) + pad_ref.shape[1:], pad_ref.dtype)
    pad_ref[:reach] = edge
    pad_ref[reach + nblk :] = edge


def stream(e_hbm, e_ref, sems):
    parts = sems.shape[0]
    per = e_ref.shape[0] // parts
    copies = []
    for i in range(parts):
        at = pl.ds(i * per, per)
        copies.append(pltpu.make_async_copy(e_hbm.at[at], e_ref.at[at], sems.at[i]))
        copies[-1].start()
    return [(c, range(i * per, (i + 1) * per)) for i, c in enumerate(copies)]


def fill_blocks(w_ref, pad_ref, reach):
    for b in range(pad_ref.shape[0] - 2 * reach):
        cols = slice(b * BLOCK, (b + 1) * BLOCK)
        block = [w_ref[c, :, cols].astype(jnp.float32) for c in range(4)]
        pad_ref[reach + b] = jnp.concatenate(block, axis=0).astype(jnp.bfloat16)


def read_code(code_ref, band, slots):
    code = [code_ref[k][0, 0] for k in range(band + slots)]
    return code[:band], code[band:]


def first_kernel(
    scale, place_ref, offs_hbm, asgs_hbm, e_hbm, w_hbm, adv_ref, img_ref, code_ref, e_all,
    pad_ref, off_ref, asg_ref, w_ref, e_sems, w_sems,
):
    e_ref = e_all.at[0]
    nblk, band = e_ref.shape[:2]
    slots = w_ref.shape[1]
    reach = band // 2
    loads = [
        pltpu.make_async_copy(w_hbm.at[:, 0], w_ref, w_sems.at[0]),
        pltpu.make_async_copy(offs_hbm, off_ref, w_sems.at[1]),
        pltpu.make_async_copy(asgs_hbm, asg_ref, w_sems.at[2]),
    ]
    for c in loads:
        c.start()
    copies = stream(e_hbm.at[0], e_ref, e_sems)
    zero_edges(pad_ref, reach)
    for c in loads:
        c.wait()
    fill_blocks(w_ref, pad_ref, reach)
    sec, me = place_ref[0][0, 0], place_ref[1][0, 0]
    offs = [off_ref[sec, k] + reach for k in range(band)]
    rows = [asg_ref[sec, j] for j in range(slots)]
    for k, value in enumerate(offs + rows + [me]):
        code_ref[k] = jnp.full(code_ref.shape[1:], value, jnp.int32)
    for c, blocks in copies:
        c.wait()
        advance_blocks(
            offs, rows, e_ref, pad_ref, adv_ref, img_ref, scale, blocks, band, slots
        )


def next_kernel(
    scale, f, code_ref, old, e_hbm, w_hbm, tok, adv_ref, img_ref, e_all,
    pad_ref, w_ref, e_sems, w_sem,
):
    e_ref = e_all.at[f]
    load = pltpu.make_async_copy(w_hbm.at[:, f], w_ref, w_sem.at[0])
    load.start()
    copies = stream(e_hbm.at[f], e_ref, e_sems)
    nblk, band = e_ref.shape[:2]
    reach = band // 2
    slots = img_ref.shape[0]
    offs, rows = read_code(code_ref, band, slots)
    zero_edges(pad_ref, reach)
    load.wait()
    fill_blocks(w_ref, pad_ref, reach)
    for c, blocks in copies:
        c.wait()
        advance_blocks(
            offs, rows, e_ref, pad_ref, adv_ref, img_ref, scale, blocks, band, slots
        )


def step_kernel(scale, f, code_ref, e_ref, w_ref, adv_ref, img_ref, pad_ref):
    nblk, band = e_ref.shape[1:3]
    reach = band // 2
    slots = img_ref.shape[0]
    offs, rows = read_code(code_ref, band, slots)
    zero_edges(pad_ref, reach)
    pad_ref[reach : reach + nblk] = w_ref[...]
    advance_blocks(
        offs, rows, e_ref.at[f], pad_ref, adv_ref, img_ref, scale, range(nblk), band, slots
    )


def pair_kernel(freqs, code_ref, *refs):
    ins, (keep_ref, send_ref) = refs[:-2], refs[-2:]
    side = code_ref[code_ref.shape[0] - 1][0, 0] & 1
    halves, rounds = keep_ref.shape[:2]
    for half in range(halves):
        for out, row in ((keep_ref, 2 * half + side), (send_ref, 2 * half + 1 - side)):
            for r in range(rounds):
                value = ins[r * freqs][row]
                for f in range(1, freqs):
                    value += ins[r * freqs + f][row]
                out[half, r] = value.astype(out.dtype)


def spread_kernel(code_ref, kept_ref, came_ref, *outs):
    mine = code_ref[code_ref.shape[0] - 1][0, 0] >> 1
    for mask, out in enumerate(outs):
        row = mine ^ mask
        out[...] = (kept_ref[row] + came_ref[row].astype(jnp.float32)).astype(out.dtype)


VMEM = pl.BlockSpec(memory_space=pltpu.VMEM)
HBM = pl.BlockSpec(memory_space=pltpu.HBM)
ANY = pl.BlockSpec(memory_space=pl.ANY)


def held(x, space):
    return pltpu.with_memory_space_constraint(x, space)


def cost(e_shape, rows):
    macs = math.prod(e_shape) * rows
    return pl.CostEstimate(flops=2 * macs, bytes_accessed=BLOCK, transcendentals=0)


def run_first(place, offsets, assign, extrap, fronts, scale):
    nblk, band = extrap.shape[1:3]
    nfield, freqs, slots, points = fronts.shape
    rows = nfield * slots
    parts = math.gcd(PARTS, nblk)
    return pl.pallas_call(
        functools.partial(first_kernel, scale),
        out_shape=(
            pltpu.VMEM((nblk, rows, BLOCK), jnp.bfloat16),
            pltpu.VMEM((slots, nblk, BLOCK), jnp.float32),
            pltpu.VMEM((band + slots + 1, 8, BLOCK), jnp.int32),
            pltpu.VMEM(extrap.shape, extrap.dtype),
        ),
        in_specs=[VMEM, HBM, HBM, HBM, HBM],
        out_specs=(VMEM,) * 4,
        scratch_shapes=[
            pltpu.VMEM((nblk + 2 * (band // 2), rows, BLOCK), jnp.bfloat16),
            pltpu.SMEM(offsets.shape, jnp.int32),
            pltpu.SMEM(assign.shape, jnp.int32),
            pltpu.VMEM((nfield, slots, points), fronts.dtype),
            pltpu.SemaphoreType.DMA((parts,)),
            pltpu.SemaphoreType.DMA((3,)),
        ],
        compiler_params=pltpu.CompilerParams(vmem_limit_bytes=4 * 2**20),
        cost_estimate=cost(extrap.shape[1:], rows),
        name="first",
    )(held(place, pltpu.VMEM), *[held(x, pltpu.HBM) for x in (offsets, assign, extrap, fronts)])


def run_next(f, code, e, extrap, fronts, token, scale):
    nblk, band = e.shape[1:3]
    nfield, freqs, slots, points = fronts.shape
    rows = nfield * slots
    parts = math.gcd(PARTS, nblk)
    return pl.pallas_call(
        functools.partial(next_kernel, scale, f),
        out_shape=(
            pltpu.VMEM((nblk, rows, BLOCK), jnp.bfloat16),
            pltpu.VMEM((slots, nblk, BLOCK), jnp.float32),
            pltpu.VMEM(e.shape, e.dtype),
        ),
        in_specs=[VMEM, VMEM, HBM, HBM, ANY],
        out_specs=(VMEM,) * 3,
        scratch_shapes=[
            pltpu.VMEM((nblk + 2 * (band // 2), rows, BLOCK), jnp.bfloat16),
            pltpu.VMEM((nfield, slots, points), fronts.dtype),
            pltpu.SemaphoreType.DMA((parts,)),
            pltpu.SemaphoreType.DMA((1,)),
        ],
        input_output_aliases={1: 2},
        compiler_params=pltpu.CompilerParams(vmem_limit_bytes=4 * 2**20),
        cost_estimate=cost(e.shape[1:], rows),
        name="next",
    )(held(code, pltpu.VMEM), held(e, pltpu.VMEM), held(extrap, pltpu.HBM), held(fronts, pltpu.HBM), token)


def run_step(f, code, e, w, scale):
    nblk, band = e.shape[1:3]
    rows = w.shape[1]
    return pl.pallas_call(
        functools.partial(step_kernel, scale, f),
        out_shape=(
            pltpu.VMEM((nblk, rows, BLOCK), jnp.bfloat16),
            pltpu.VMEM((rows // 4, nblk, BLOCK), jnp.float32),
        ),
        in_specs=[VMEM, VMEM, VMEM],
        out_specs=(VMEM, VMEM),
        scratch_shapes=[pltpu.VMEM((nblk + 2 * (band // 2), rows, BLOCK), jnp.bfloat16)],
        compiler_params=pltpu.CompilerParams(vmem_limit_bytes=4 * 2**20),
        cost_estimate=cost(e.shape[1:], rows),
        name="step",
    )(*[held(x, pltpu.VMEM) for x in (code, e, w)])


def fold_owners(code, parts, rounds, owners):
    size = lax.axis_size("depth")
    rows, nblk, lanes = parts[0].shape
    left = owners // 2
    half = (left, rounds, nblk, lanes)
    small = pl.CostEstimate(flops=BLOCK, bytes_accessed=BLOCK, transcendentals=0)
    keep, send = pl.pallas_call(
        functools.partial(pair_kernel, len(parts) // rounds),
        out_shape=(pltpu.VMEM(half, jnp.float32), pltpu.VMEM(half, jnp.bfloat16)),
        in_specs=[VMEM] * (1 + len(parts)),
        out_specs=(VMEM, VMEM),
        compiler_params=pltpu.CompilerParams(vmem_limit_bytes=4 * 2**20),
        cost_estimate=small,
        name="pair",
    )(*[held(x, pltpu.VMEM) for x in (code, *parts)])
    came = lax.ppermute(send, "depth", [(i, i ^ 1) for i in range(size)])
    own, *others = pl.pallas_call(
        spread_kernel,
        out_shape=tuple(
            pltpu.VMEM(half[1:], jnp.bfloat16 if mask else jnp.float32) for mask in range(left)
        ),
        in_specs=[VMEM] * 3,
        out_specs=(VMEM,) * left,
        compiler_params=pltpu.CompilerParams(vmem_limit_bytes=4 * 2**20),
        cost_estimate=small,
        name="spread",
    )(*[held(x, pltpu.VMEM) for x in (code, keep, came)])
    for mask, other in enumerate(others, 1):
        other = lax.ppermute(other, "depth", [(i, i ^ (2 * mask)) for i in range(size)])
        own = own + other.astype(jnp.float32)
    return own


def on_device(fronts, extrap, offsets, assign):
    sections = offsets.shape[0]
    size = lax.axis_size("depth")
    owners = size // sections
    index = lax.axis_index("depth")
    place = jnp.stack([lax.div(index, owners), lax.rem(index, owners)]).astype(jnp.int32)
    place = jnp.broadcast_to(place[:, None, None], (2, 8, BLOCK))
    nfield, freqs, slots, points = fronts.shape
    nblk = extrap.shape[1]
    scale = 1.0 / math.sqrt(2.0 * owners * freqs)
    onward = [(i, (i + owners) % size) for i in range(size)]
    waves, parts = [None] * freqs, []
    for r in range(HANDOVERS):
        for f in range(freqs):
            if r == 0 and f == 0:
                adv, img, code, e = run_first(place, offsets, assign, extrap, fronts, scale)
                token = lax.ppermute(img[:1], "depth", [(i, i ^ 1) for i in range(size)])
            elif r == 0:
                adv, img, e = run_next(f, code, e, extrap, fronts, token, scale)
            else:
                adv, img = run_step(f, code, e, waves[f], scale)
            parts.append(img)
            waves[f] = lax.ppermute(adv, "depth", onward) if r + 1 < HANDOVERS else adv
    images = fold_owners(code, parts, HANDOVERS, owners).reshape(HANDOVERS, 1, points)
    last = jnp.stack(waves).reshape(freqs, nblk, nfield, slots, BLOCK)
    last = last.transpose(2, 0, 3, 1, 4).reshape(fronts.shape)
    return images, last


def solution(mesh):
    placed = (
        P(None, ("groups", "depth"), None, None),
        P("depth", None, None, None, None, None),
        P(),
        P(),
    )
    return jax.shard_map(
        on_device,
        mesh=mesh,
        in_specs=placed,
        out_specs=(P(None, ("groups", "depth"), None), P(None, ("groups", "depth"), None, None)),
        check_vma=False,
    )
```

```python
import functools
import math

import jax
import jax.numpy as jnp
from jax import lax
from jax.experimental import pallas as pl
from jax.experimental.pallas import tpu as pltpu
from jax.sharding import PartitionSpec as P

BLOCK = 128
HANDOVERS = 8
ORDER = (3, 2, 1)
PARTS = 4


def advance_blocks(offs, rows, e_ref, pad_ref, adv_ref, img_ref, scale, blocks, band, slots):
    for b in blocks:
        lhs = jnp.concatenate([pad_ref[b + offs[k]] for k in range(band)], axis=1)
        er = e_ref[b, :, 0].reshape(band * BLOCK, BLOCK)
        ei = e_ref[b, :, 1].reshape(band * BLOCK, BLOCK)
        p = jnp.dot(lhs, er, preferred_element_type=jnp.float32)
        q = jnp.dot(lhs, ei, preferred_element_type=jnp.float32)
        p = [p[c * slots : (c + 1) * slots] for c in range(4)]
        q = [q[c * slots : (c + 1) * slots] for c in range(4)]
        new = jnp.concatenate([p[0] - q[1], q[0] + p[1], p[2] + q[3], p[3] - q[2]], axis=0)
        new = new.astype(jnp.bfloat16)
        adv_ref[b] = new
        f = new.astype(jnp.float32)
        f = [f[c * slots : (c + 1) * slots] for c in range(4)]
        part = scale * (f[0] * f[2] + f[1] * f[3])
        for j in range(slots):
            at = (pl.ds(rows[j], 1), b)
            img_ref[at] = part[j : j + 1]


def zero_edges(pad_ref, reach):
    nblk = pad_ref.shape[0] - 2 * reach
    edge = jnp.zeros((reach,) + pad_ref.shape[1:], pad_ref.dtype)
    pad_ref[:reach] = edge
    pad_ref[reach + nblk :] = edge


def stream(e_hbm, e_ref, sems):
    parts = sems.shape[0]
    per = e_ref.shape[0] // parts
    copies = []
    for i in range(parts):
        at = pl.ds(i * per, per)
        copies.append(pltpu.make_async_copy(e_hbm.at[at], e_ref.at[at], sems.at[i]))
        copies[-1].start()
    return [(c, range(i * per, (i + 1) * per)) for i, c in enumerate(copies)]


def fill_blocks(w_ref, pad_ref, reach):
    for b in range(pad_ref.shape[0] - 2 * reach):
        cols = slice(b * BLOCK, (b + 1) * BLOCK)
        block = [w_ref[c, :, cols].astype(jnp.float32) for c in range(4)]
        pad_ref[reach + b] = jnp.concatenate(block, axis=0).astype(jnp.bfloat16)


def read_code(code_ref, band, slots):
    code = [code_ref[k][0, 0] for k in range(band + slots)]
    return code[:band], code[band:]


def first_kernel(
    scale, place_ref, offs_hbm, asgs_hbm, e_hbm, w_hbm, adv_ref, img_ref, code_ref, e_all,
    pad_ref, off_ref, asg_ref, w_ref, e_sems, w_sems,
):
    e_ref = e_all.at[0]
    nblk, band = e_ref.shape[:2]
    slots = w_ref.shape[1]
    reach = band // 2
    loads = [
        pltpu.make_async_copy(w_hbm.at[:, 0], w_ref, w_sems.at[0]),
        pltpu.make_async_copy(offs_hbm, off_ref, w_sems.at[1]),
        pltpu.make_async_copy(asgs_hbm, asg_ref, w_sems.at[2]),
    ]
    for c in loads:
        c.start()
    copies = stream(e_hbm.at[0], e_ref, e_sems)
    zero_edges(pad_ref, reach)
    for c in loads:
        c.wait()
    fill_blocks(w_ref, pad_ref, reach)
    sec, me = place_ref[0][0, 0], place_ref[1][0, 0]
    offs = [off_ref[sec, k] + reach for k in range(band)]
    rows = [asg_ref[sec, j] for j in range(slots)]
    for k, value in enumerate(offs + rows + [me]):
        code_ref[k] = jnp.full(code_ref.shape[1:], value, jnp.int32)
    for c, blocks in copies:
        c.wait()
        advance_blocks(
            offs, rows, e_ref, pad_ref, adv_ref, img_ref, scale, blocks, band, slots
        )


def next_kernel(
    scale, f, code_ref, old, e_hbm, w_hbm, tok, adv_ref, img_ref, e_all,
    pad_ref, w_ref, e_sems, w_sem,
):
    e_ref = e_all.at[f]
    load = pltpu.make_async_copy(w_hbm.at[:, f], w_ref, w_sem.at[0])
    load.start()
    copies = stream(e_hbm.at[f], e_ref, e_sems)
    nblk, band = e_ref.shape[:2]
    reach = band // 2
    slots = img_ref.shape[0]
    offs, rows = read_code(code_ref, band, slots)
    zero_edges(pad_ref, reach)
    load.wait()
    fill_blocks(w_ref, pad_ref, reach)
    for c, blocks in copies:
        c.wait()
        advance_blocks(
            offs, rows, e_ref, pad_ref, adv_ref, img_ref, scale, blocks, band, slots
        )


def step_kernel(scale, f, code_ref, e_ref, w_ref, adv_ref, img_ref, pad_ref):
    nblk, band = e_ref.shape[1:3]
    reach = band // 2
    slots = img_ref.shape[0]
    offs, rows = read_code(code_ref, band, slots)
    zero_edges(pad_ref, reach)
    pad_ref[reach : reach + nblk] = w_ref[...]
    advance_blocks(
        offs, rows, e_ref.at[f], pad_ref, adv_ref, img_ref, scale, range(nblk), band, slots
    )


def pair_kernel(freqs, code_ref, *refs):
    ins, (keep_ref, send_ref) = refs[:-2], refs[-2:]
    side = code_ref[code_ref.shape[0] - 1][0, 0] & 1
    halves, rounds = keep_ref.shape[:2]
    for half in range(halves):
        for out, row in ((keep_ref, 2 * half + side), (send_ref, 2 * half + 1 - side)):
            for r in range(rounds):
                value = ins[r * freqs][row]
                for f in range(1, freqs):
                    value += ins[r * freqs + f][row]
                out[half, r] = value.astype(out.dtype)


def spread_kernel(code_ref, kept_ref, came_ref, *outs):
    mine = code_ref[code_ref.shape[0] - 1][0, 0] >> 1
    for mask, out in enumerate(outs):
        row = mine ^ mask
        out[...] = (kept_ref[row] + came_ref[row].astype(jnp.float32)).astype(out.dtype)


VMEM = pl.BlockSpec(memory_space=pltpu.VMEM)
HBM = pl.BlockSpec(memory_space=pltpu.HBM)
ANY = pl.BlockSpec(memory_space=pl.ANY)


def held(x, space):
    return pltpu.with_memory_space_constraint(x, space)


def cost(e_shape, rows):
    macs = math.prod(e_shape) * rows
    return pl.CostEstimate(flops=2 * macs, bytes_accessed=BLOCK, transcendentals=0)


def run_first(place, offsets, assign, extrap, fronts, scale):
    nblk, band = extrap.shape[1:3]
    nfield, freqs, slots, points = fronts.shape
    rows = nfield * slots
    parts = math.gcd(PARTS, nblk)
    return pl.pallas_call(
        functools.partial(first_kernel, scale),
        out_shape=(
            pltpu.VMEM((nblk, rows, BLOCK), jnp.bfloat16),
            pltpu.VMEM((slots, nblk, BLOCK), jnp.float32),
            pltpu.VMEM((band + slots + 1, 8, BLOCK), jnp.int32),
            pltpu.VMEM(extrap.shape, extrap.dtype),
        ),
        in_specs=[VMEM, HBM, HBM, HBM, HBM],
        out_specs=(VMEM,) * 4,
        scratch_shapes=[
            pltpu.VMEM((nblk + 2 * (band // 2), rows, BLOCK), jnp.bfloat16),
            pltpu.SMEM(offsets.shape, jnp.int32),
            pltpu.SMEM(assign.shape, jnp.int32),
            pltpu.VMEM((nfield, slots, points), fronts.dtype),
            pltpu.SemaphoreType.DMA((parts,)),
            pltpu.SemaphoreType.DMA((3,)),
        ],
        compiler_params=pltpu.CompilerParams(vmem_limit_bytes=4 * 2**20),
        cost_estimate=cost(extrap.shape[1:], rows),
        name="first",
    )(held(place, pltpu.VMEM), *[held(x, pltpu.HBM) for x in (offsets, assign, extrap, fronts)])


def run_next(f, code, e, extrap, fronts, token, scale):
    nblk, band = e.shape[1:3]
    nfield, freqs, slots, points = fronts.shape
    rows = nfield * slots
    parts = math.gcd(PARTS, nblk)
    return pl.pallas_call(
        functools.partial(next_kernel, scale, f),
        out_shape=(
            pltpu.VMEM((nblk, rows, BLOCK), jnp.bfloat16),
            pltpu.VMEM((slots, nblk, BLOCK), jnp.float32),
            pltpu.VMEM(e.shape, e.dtype),
        ),
        in_specs=[VMEM, VMEM, HBM, HBM, ANY],
        out_specs=(VMEM,) * 3,
        scratch_shapes=[
            pltpu.VMEM((nblk + 2 * (band // 2), rows, BLOCK), jnp.bfloat16),
            pltpu.VMEM((nfield, slots, points), fronts.dtype),
            pltpu.SemaphoreType.DMA((parts,)),
            pltpu.SemaphoreType.DMA((1,)),
        ],
        input_output_aliases={1: 2},
        compiler_params=pltpu.CompilerParams(vmem_limit_bytes=4 * 2**20),
        cost_estimate=cost(e.shape[1:], rows),
        name="next",
    )(held(code, pltpu.VMEM), held(e, pltpu.VMEM), held(extrap, pltpu.HBM), held(fronts, pltpu.HBM), token)


def run_step(f, code, e, w, scale):
    nblk, band = e.shape[1:3]
    rows = w.shape[1]
    return pl.pallas_call(
        functools.partial(step_kernel, scale, f),
        out_shape=(
            pltpu.VMEM((nblk, rows, BLOCK), jnp.bfloat16),
            pltpu.VMEM((rows // 4, nblk, BLOCK), jnp.float32),
        ),
        in_specs=[VMEM, VMEM, VMEM],
        out_specs=(VMEM, VMEM),
        scratch_shapes=[pltpu.VMEM((nblk + 2 * (band // 2), rows, BLOCK), jnp.bfloat16)],
        compiler_params=pltpu.CompilerParams(vmem_limit_bytes=4 * 2**20),
        cost_estimate=cost(e.shape[1:], rows),
        name="step",
    )(*[held(x, pltpu.VMEM) for x in (code, e, w)])


def fold_owners(code, parts, rounds, owners):
    size = lax.axis_size("depth")
    rows, nblk, lanes = parts[0].shape
    left = owners // 2
    half = (left, rounds, nblk, lanes)
    small = pl.CostEstimate(flops=BLOCK, bytes_accessed=BLOCK, transcendentals=0)
    keep, send = pl.pallas_call(
        functools.partial(pair_kernel, len(parts) // rounds),
        out_shape=(pltpu.VMEM(half, jnp.float32), pltpu.VMEM(half, jnp.bfloat16)),
        in_specs=[VMEM] * (1 + len(parts)),
        out_specs=(VMEM, VMEM),
        compiler_params=pltpu.CompilerParams(vmem_limit_bytes=4 * 2**20),
        cost_estimate=small,
        name="pair",
    )(*[held(x, pltpu.VMEM) for x in (code, *parts)])
    came = lax.ppermute(send, "depth", [(i, i ^ 1) for i in range(size)])
    own, *others = pl.pallas_call(
        spread_kernel,
        out_shape=tuple(
            pltpu.VMEM(half[1:], jnp.bfloat16 if mask else jnp.float32) for mask in range(left)
        ),
        in_specs=[VMEM] * 3,
        out_specs=(VMEM,) * left,
        compiler_params=pltpu.CompilerParams(vmem_limit_bytes=4 * 2**20),
        cost_estimate=small,
        name="spread",
    )(*[held(x, pltpu.VMEM) for x in (code, keep, came)])
    for mask in ORDER:
        other = lax.ppermute(others[mask - 1], "depth", [(i, i ^ (2 * mask)) for i in range(size)])
        own = own + other.astype(jnp.float32)
    return own


def on_device(fronts, extrap, offsets, assign):
    sections = offsets.shape[0]
    size = lax.axis_size("depth")
    owners = size // sections
    index = lax.axis_index("depth")
    place = jnp.stack([lax.div(index, owners), lax.rem(index, owners)]).astype(jnp.int32)
    place = jnp.broadcast_to(place[:, None, None], (2, 8, BLOCK))
    nfield, freqs, slots, points = fronts.shape
    nblk = extrap.shape[1]
    scale = 1.0 / math.sqrt(2.0 * owners * freqs)
    onward = [(i, (i + owners) % size) for i in range(size)]
    waves, parts = [None] * freqs, []
    for r in range(HANDOVERS):
        for f in range(freqs):
            if r == 0 and f == 0:
                adv, img, code, e = run_first(place, offsets, assign, extrap, fronts, scale)
                token = lax.ppermute(img[:1], "depth", [(i, i ^ 1) for i in range(size)])
            elif r == 0:
                adv, img, e = run_next(f, code, e, extrap, fronts, token, scale)
            else:
                adv, img = run_step(f, code, e, waves[f], scale)
            parts.append(img)
            waves[f] = lax.ppermute(adv, "depth", onward) if r + 1 < HANDOVERS else adv
    images = fold_owners(code, parts, HANDOVERS, owners).reshape(HANDOVERS, 1, points)
    last = jnp.stack(waves).reshape(freqs, nblk, nfield, slots, BLOCK)
    last = last.transpose(2, 0, 3, 1, 4).reshape(fronts.shape)
    return images, last


def solution(mesh):
    placed = (
        P(None, ("groups", "depth"), None, None),
        P("depth", None, None, None, None, None),
        P(),
        P(),
    )
    return jax.shard_map(
        on_device,
        mesh=mesh,
        in_specs=placed,
        out_specs=(P(None, ("groups", "depth"), None), P(None, ("groups", "depth"), None, None)),
        check_vma=False,
    )
```

```python
import functools
import math

import jax
import jax.numpy as jnp
from jax import lax
from jax.experimental import pallas as pl
from jax.experimental.pallas import tpu as pltpu
from jax.sharding import PartitionSpec as P

BLOCK = 128
HANDOVERS = 8
ORDER = (3, 2, 1)
PARTS = 4


def advance_blocks(offs, rows, e_ref, pad_ref, adv_ref, img_ref, scale, blocks, band, slots):
    for b in blocks:
        both = 0.0
        for k in range(band):
            planes = jnp.concatenate([e_ref[b, k, 0], e_ref[b, k, 1]], axis=1)
            both += jnp.dot(pad_ref[b + offs[k]], planes, preferred_element_type=jnp.float32)
        p, q = both[:, :BLOCK], both[:, BLOCK:]
        p = [p[c * slots : (c + 1) * slots] for c in range(4)]
        q = [q[c * slots : (c + 1) * slots] for c in range(4)]
        new = jnp.concatenate([p[0] - q[1], q[0] + p[1], p[2] + q[3], p[3] - q[2]], axis=0)
        new = new.astype(jnp.bfloat16)
        adv_ref[b] = new
        f = new.astype(jnp.float32)
        f = [f[c * slots : (c + 1) * slots] for c in range(4)]
        part = scale * (f[0] * f[2] + f[1] * f[3])
        for j in range(slots):
            at = (pl.ds(rows[j], 1), b)
            img_ref[at] = part[j : j + 1]


def zero_edges(pad_ref, reach):
    nblk = pad_ref.shape[0] - 2 * reach
    edge = jnp.zeros((reach,) + pad_ref.shape[1:], pad_ref.dtype)
    pad_ref[:reach] = edge
    pad_ref[reach + nblk :] = edge


def stream(e_hbm, e_ref, sems):
    parts = sems.shape[0]
    per = e_ref.shape[0] // parts
    copies = []
    for i in range(parts):
        at = pl.ds(i * per, per)
        copies.append(pltpu.make_async_copy(e_hbm.at[at], e_ref.at[at], sems.at[i]))
        copies[-1].start()
    return [(c, range(i * per, (i + 1) * per)) for i, c in enumerate(copies)]


def fill_blocks(w_ref, pad_ref, reach):
    for b in range(pad_ref.shape[0] - 2 * reach):
        cols = slice(b * BLOCK, (b + 1) * BLOCK)
        block = [w_ref[c, :, cols].astype(jnp.float32) for c in range(4)]
        pad_ref[reach + b] = jnp.concatenate(block, axis=0).astype(jnp.bfloat16)


def read_code(code_ref, band, slots):
    code = [code_ref[k][0, 0] for k in range(band + slots)]
    return code[:band], code[band:]


def first_kernel(
    scale, place_ref, offs_hbm, asgs_hbm, e_hbm, w_hbm, adv_ref, img_ref, code_ref, e_all,
    pad_ref, off_ref, asg_ref, w_ref, e_sems, w_sems,
):
    e_ref = e_all.at[0]
    nblk, band = e_ref.shape[:2]
    slots = w_ref.shape[1]
    reach = band // 2
    loads = [
        pltpu.make_async_copy(w_hbm.at[:, 0], w_ref, w_sems.at[0]),
        pltpu.make_async_copy(offs_hbm, off_ref, w_sems.at[1]),
        pltpu.make_async_copy(asgs_hbm, asg_ref, w_sems.at[2]),
    ]
    for c in loads:
        c.start()
    copies = stream(e_hbm.at[0], e_ref, e_sems)
    zero_edges(pad_ref, reach)
    for c in loads:
        c.wait()
    fill_blocks(w_ref, pad_ref, reach)
    sec, me = place_ref[0][0, 0], place_ref[1][0, 0]
    offs = [off_ref[sec, k] + reach for k in range(band)]
    rows = [asg_ref[sec, j] for j in range(slots)]
    for k, value in enumerate(offs + rows + [me]):
        code_ref[k] = jnp.full(code_ref.shape[1:], value, jnp.int32)
    for c, blocks in copies:
        c.wait()
        advance_blocks(
            offs, rows, e_ref, pad_ref, adv_ref, img_ref, scale, blocks, band, slots
        )


def next_kernel(
    scale, f, code_ref, old, e_hbm, w_hbm, tok, adv_ref, img_ref, e_all,
    pad_ref, w_ref, e_sems, w_sem,
):
    e_ref = e_all.at[f]
    load = pltpu.make_async_copy(w_hbm.at[:, f], w_ref, w_sem.at[0])
    load.start()
    copies = stream(e_hbm.at[f], e_ref, e_sems)
    nblk, band = e_ref.shape[:2]
    reach = band // 2
    slots = img_ref.shape[0]
    offs, rows = read_code(code_ref, band, slots)
    zero_edges(pad_ref, reach)
    load.wait()
    fill_blocks(w_ref, pad_ref, reach)
    for c, blocks in copies:
        c.wait()
        advance_blocks(
            offs, rows, e_ref, pad_ref, adv_ref, img_ref, scale, blocks, band, slots
        )


def step_kernel(scale, f, code_ref, e_ref, w_ref, adv_ref, img_ref, pad_ref):
    nblk, band = e_ref.shape[1:3]
    reach = band // 2
    slots = img_ref.shape[0]
    offs, rows = read_code(code_ref, band, slots)
    zero_edges(pad_ref, reach)
    pad_ref[reach : reach + nblk] = w_ref[...]
    advance_blocks(
        offs, rows, e_ref.at[f], pad_ref, adv_ref, img_ref, scale, range(nblk), band, slots
    )


def pair_kernel(freqs, code_ref, *refs):
    ins, (keep_ref, send_ref) = refs[:-2], refs[-2:]
    side = code_ref[code_ref.shape[0] - 1][0, 0] & 1
    halves, rounds = keep_ref.shape[:2]
    for half in range(halves):
        for out, row in ((keep_ref, 2 * half + side), (send_ref, 2 * half + 1 - side)):
            for r in range(rounds):
                value = ins[r * freqs][row]
                for f in range(1, freqs):
                    value += ins[r * freqs + f][row]
                out[half, r] = value.astype(out.dtype)


def spread_kernel(code_ref, kept_ref, came_ref, *outs):
    mine = code_ref[code_ref.shape[0] - 1][0, 0] >> 1
    for mask, out in enumerate(outs):
        row = mine ^ mask
        out[...] = (kept_ref[row] + came_ref[row].astype(jnp.float32)).astype(out.dtype)


VMEM = pl.BlockSpec(memory_space=pltpu.VMEM)
HBM = pl.BlockSpec(memory_space=pltpu.HBM)
ANY = pl.BlockSpec(memory_space=pl.ANY)


def held(x, space):
    return pltpu.with_memory_space_constraint(x, space)


def cost(e_shape, rows):
    macs = math.prod(e_shape) * rows
    return pl.CostEstimate(flops=2 * macs, bytes_accessed=BLOCK, transcendentals=0)


def run_first(place, offsets, assign, extrap, fronts, scale):
    nblk, band = extrap.shape[1:3]
    nfield, freqs, slots, points = fronts.shape
    rows = nfield * slots
    parts = math.gcd(PARTS, nblk)
    return pl.pallas_call(
        functools.partial(first_kernel, scale),
        out_shape=(
            pltpu.VMEM((nblk, rows, BLOCK), jnp.bfloat16),
            pltpu.VMEM((slots, nblk, BLOCK), jnp.float32),
            pltpu.VMEM((band + slots + 1, 8, BLOCK), jnp.int32),
            pltpu.VMEM(extrap.shape, extrap.dtype),
        ),
        in_specs=[VMEM, HBM, HBM, HBM, HBM],
        out_specs=(VMEM,) * 4,
        scratch_shapes=[
            pltpu.VMEM((nblk + 2 * (band // 2), rows, BLOCK), jnp.bfloat16),
            pltpu.SMEM(offsets.shape, jnp.int32),
            pltpu.SMEM(assign.shape, jnp.int32),
            pltpu.VMEM((nfield, slots, points), fronts.dtype),
            pltpu.SemaphoreType.DMA((parts,)),
            pltpu.SemaphoreType.DMA((3,)),
        ],
        compiler_params=pltpu.CompilerParams(vmem_limit_bytes=4 * 2**20),
        cost_estimate=cost(extrap.shape[1:], rows),
        name="first",
    )(held(place, pltpu.VMEM), *[held(x, pltpu.HBM) for x in (offsets, assign, extrap, fronts)])


def run_next(f, code, e, extrap, fronts, token, scale):
    nblk, band = e.shape[1:3]
    nfield, freqs, slots, points = fronts.shape
    rows = nfield * slots
    parts = math.gcd(PARTS, nblk)
    return pl.pallas_call(
        functools.partial(next_kernel, scale, f),
        out_shape=(
            pltpu.VMEM((nblk, rows, BLOCK), jnp.bfloat16),
            pltpu.VMEM((slots, nblk, BLOCK), jnp.float32),
            pltpu.VMEM(e.shape, e.dtype),
        ),
        in_specs=[VMEM, VMEM, HBM, HBM, ANY],
        out_specs=(VMEM,) * 3,
        scratch_shapes=[
            pltpu.VMEM((nblk + 2 * (band // 2), rows, BLOCK), jnp.bfloat16),
            pltpu.VMEM((nfield, slots, points), fronts.dtype),
            pltpu.SemaphoreType.DMA((parts,)),
            pltpu.SemaphoreType.DMA((1,)),
        ],
        input_output_aliases={1: 2},
        compiler_params=pltpu.CompilerParams(vmem_limit_bytes=4 * 2**20),
        cost_estimate=cost(e.shape[1:], rows),
        name="next",
    )(held(code, pltpu.VMEM), held(e, pltpu.VMEM), held(extrap, pltpu.HBM), held(fronts, pltpu.HBM), token)


def run_step(f, code, e, w, scale):
    nblk, band = e.shape[1:3]
    rows = w.shape[1]
    return pl.pallas_call(
        functools.partial(step_kernel, scale, f),
        out_shape=(
            pltpu.VMEM((nblk, rows, BLOCK), jnp.bfloat16),
            pltpu.VMEM((rows // 4, nblk, BLOCK), jnp.float32),
        ),
        in_specs=[VMEM, VMEM, VMEM],
        out_specs=(VMEM, VMEM),
        scratch_shapes=[pltpu.VMEM((nblk + 2 * (band // 2), rows, BLOCK), jnp.bfloat16)],
        compiler_params=pltpu.CompilerParams(vmem_limit_bytes=4 * 2**20),
        cost_estimate=cost(e.shape[1:], rows),
        name="step",
    )(*[held(x, pltpu.VMEM) for x in (code, e, w)])


def fold_owners(code, parts, rounds, owners):
    size = lax.axis_size("depth")
    rows, nblk, lanes = parts[0].shape
    left = owners // 2
    half = (left, rounds, nblk, lanes)
    small = pl.CostEstimate(flops=BLOCK, bytes_accessed=BLOCK, transcendentals=0)
    keep, send = pl.pallas_call(
        functools.partial(pair_kernel, len(parts) // rounds),
        out_shape=(pltpu.VMEM(half, jnp.float32), pltpu.VMEM(half, jnp.bfloat16)),
        in_specs=[VMEM] * (1 + len(parts)),
        out_specs=(VMEM, VMEM),
        compiler_params=pltpu.CompilerParams(vmem_limit_bytes=4 * 2**20),
        cost_estimate=small,
        name="pair",
    )(*[held(x, pltpu.VMEM) for x in (code, *parts)])
    came = lax.ppermute(send, "depth", [(i, i ^ 1) for i in range(size)])
    own, *others = pl.pallas_call(
        spread_kernel,
        out_shape=tuple(
            pltpu.VMEM(half[1:], jnp.bfloat16 if mask else jnp.float32) for mask in range(left)
        ),
        in_specs=[VMEM] * 3,
        out_specs=(VMEM,) * left,
        compiler_params=pltpu.CompilerParams(vmem_limit_bytes=4 * 2**20),
        cost_estimate=small,
        name="spread",
    )(*[held(x, pltpu.VMEM) for x in (code, keep, came)])
    for mask in ORDER:
        other = lax.ppermute(others[mask - 1], "depth", [(i, i ^ (2 * mask)) for i in range(size)])
        own = own + other.astype(jnp.float32)
    return own


def on_device(fronts, extrap, offsets, assign):
    sections = offsets.shape[0]
    size = lax.axis_size("depth")
    owners = size // sections
    index = lax.axis_index("depth")
    place = jnp.stack([lax.div(index, owners), lax.rem(index, owners)]).astype(jnp.int32)
    place = jnp.broadcast_to(place[:, None, None], (2, 8, BLOCK))
    nfield, freqs, slots, points = fronts.shape
    nblk = extrap.shape[1]
    scale = 1.0 / math.sqrt(2.0 * owners * freqs)
    onward = [(i, (i + owners) % size) for i in range(size)]
    waves, parts = [None] * freqs, []
    for r in range(HANDOVERS):
        for f in range(freqs):
            if r == 0 and f == 0:
                adv, img, code, e = run_first(place, offsets, assign, extrap, fronts, scale)
                token = lax.ppermute(img[:1], "depth", [(i, i ^ 1) for i in range(size)])
            elif r == 0:
                adv, img, e = run_next(f, code, e, extrap, fronts, token, scale)
            else:
                adv, img = run_step(f, code, e, waves[f], scale)
            parts.append(img)
            waves[f] = lax.ppermute(adv, "depth", onward) if r + 1 < HANDOVERS else adv
    images = fold_owners(code, parts, HANDOVERS, owners).reshape(HANDOVERS, 1, points)
    last = jnp.stack(waves).reshape(freqs, nblk, nfield, slots, BLOCK)
    last = last.transpose(2, 0, 3, 1, 4).reshape(fronts.shape)
    return images, last


def solution(mesh):
    placed = (
        P(None, ("groups", "depth"), None, None),
        P("depth", None, None, None, None, None),
        P(),
        P(),
    )
    return jax.shard_map(
        on_device,
        mesh=mesh,
        in_specs=placed,
        out_specs=(P(None, ("groups", "depth"), None), P(None, ("groups", "depth"), None, None)),
        check_vma=False,
    )
```

```python
import functools
import math

import jax
import jax.numpy as jnp
from jax import lax
from jax.experimental import pallas as pl
from jax.experimental.pallas import tpu as pltpu
from jax.sharding import PartitionSpec as P

BLOCK = 128
HANDOVERS = 8
ORDER = (3, 2, 1)
PARTS = 4


def advance_blocks(offs, rows, e_ref, pad_ref, adv_ref, img_ref, scale, blocks, band, slots):
    for b in blocks:
        both = None
        for k in range(band):
            planes = jnp.concatenate([e_ref[b, k, 0], e_ref[b, k, 1]], axis=1)
            part = jnp.dot(pad_ref[b + offs[k]], planes, preferred_element_type=jnp.float32)
            both = part if both is None else both + part
        p, q = both[:, :BLOCK], both[:, BLOCK:]
        p = [p[c * slots : (c + 1) * slots] for c in range(4)]
        q = [q[c * slots : (c + 1) * slots] for c in range(4)]
        new = jnp.concatenate([p[0] - q[1], q[0] + p[1], p[2] + q[3], p[3] - q[2]], axis=0)
        new = new.astype(jnp.bfloat16)
        adv_ref[b] = new
        f = new.astype(jnp.float32)
        f = [f[c * slots : (c + 1) * slots] for c in range(4)]
        part = scale * (f[0] * f[2] + f[1] * f[3])
        for j in range(slots):
            at = (pl.ds(rows[j], 1), b)
            img_ref[at] = part[j : j + 1]


def zero_edges(pad_ref, reach):
    nblk = pad_ref.shape[0] - 2 * reach
    edge = jnp.zeros((reach,) + pad_ref.shape[1:], pad_ref.dtype)
    pad_ref[:reach] = edge
    pad_ref[reach + nblk :] = edge


def stream(e_hbm, e_ref, sems):
    parts = sems.shape[0]
    per = e_ref.shape[0] // parts
    copies = []
    for i in range(parts):
        at = pl.ds(i * per, per)
        copies.append(pltpu.make_async_copy(e_hbm.at[at], e_ref.at[at], sems.at[i]))
        copies[-1].start()
    return [(c, range(i * per, (i + 1) * per)) for i, c in enumerate(copies)]


def fill_blocks(w_ref, pad_ref, reach):
    for b in range(pad_ref.shape[0] - 2 * reach):
        cols = slice(b * BLOCK, (b + 1) * BLOCK)
        block = [w_ref[c, :, cols].astype(jnp.float32) for c in range(4)]
        pad_ref[reach + b] = jnp.concatenate(block, axis=0).astype(jnp.bfloat16)


def read_code(code_ref, band, slots):
    code = [code_ref[k][0, 0] for k in range(band + slots)]
    return code[:band], code[band:]


def first_kernel(
    scale, place_ref, offs_hbm, asgs_hbm, e_hbm, w_hbm, adv_ref, img_ref, code_ref, e_all,
    pad_ref, off_ref, asg_ref, w_ref, e_sems, w_sems,
):
    e_ref = e_all.at[0]
    nblk, band = e_ref.shape[:2]
    slots = w_ref.shape[1]
    reach = band // 2
    loads = [
        pltpu.make_async_copy(w_hbm.at[:, 0], w_ref, w_sems.at[0]),
        pltpu.make_async_copy(offs_hbm, off_ref, w_sems.at[1]),
        pltpu.make_async_copy(asgs_hbm, asg_ref, w_sems.at[2]),
    ]
    for c in loads:
        c.start()
    copies = stream(e_hbm.at[0], e_ref, e_sems)
    zero_edges(pad_ref, reach)
    for c in loads:
        c.wait()
    fill_blocks(w_ref, pad_ref, reach)
    sec, me = place_ref[0][0, 0], place_ref[1][0, 0]
    offs = [off_ref[sec, k] + reach for k in range(band)]
    rows = [asg_ref[sec, j] for j in range(slots)]
    for k, value in enumerate(offs + rows + [me]):
        code_ref[k] = jnp.full(code_ref.shape[1:], value, jnp.int32)
    for c, blocks in copies:
        c.wait()
        advance_blocks(
            offs, rows, e_ref, pad_ref, adv_ref, img_ref, scale, blocks, band, slots
        )


def next_kernel(
    scale, f, code_ref, old, e_hbm, w_hbm, tok, adv_ref, img_ref, e_all,
    pad_ref, w_ref, e_sems, w_sem,
):
    e_ref = e_all.at[f]
    load = pltpu.make_async_copy(w_hbm.at[:, f], w_ref, w_sem.at[0])
    load.start()
    copies = stream(e_hbm.at[f], e_ref, e_sems)
    nblk, band = e_ref.shape[:2]
    reach = band // 2
    slots = img_ref.shape[0]
    offs, rows = read_code(code_ref, band, slots)
    zero_edges(pad_ref, reach)
    load.wait()
    fill_blocks(w_ref, pad_ref, reach)
    for c, blocks in copies:
        c.wait()
        advance_blocks(
            offs, rows, e_ref, pad_ref, adv_ref, img_ref, scale, blocks, band, slots
        )


def step_kernel(scale, f, code_ref, e_ref, w_ref, adv_ref, img_ref, pad_ref):
    nblk, band = e_ref.shape[1:3]
    reach = band // 2
    slots = img_ref.shape[0]
    offs, rows = read_code(code_ref, band, slots)
    zero_edges(pad_ref, reach)
    pad_ref[reach : reach + nblk] = w_ref[...]
    advance_blocks(
        offs, rows, e_ref.at[f], pad_ref, adv_ref, img_ref, scale, range(nblk), band, slots
    )


def pair_kernel(freqs, code_ref, *refs):
    ins, (keep_ref, send_ref) = refs[:-2], refs[-2:]
    side = code_ref[code_ref.shape[0] - 1][0, 0] & 1
    halves, rounds = keep_ref.shape[:2]
    for half in range(halves):
        for out, row in ((keep_ref, 2 * half + side), (send_ref, 2 * half + 1 - side)):
            for r in range(rounds):
                value = ins[r * freqs][row]
                for f in range(1, freqs):
                    value += ins[r * freqs + f][row]
                out[half, r] = value.astype(out.dtype)


def spread_kernel(code_ref, kept_ref, came_ref, *outs):
    mine = code_ref[code_ref.shape[0] - 1][0, 0] >> 1
    for mask, out in enumerate(outs):
        row = mine ^ mask
        out[...] = (kept_ref[row] + came_ref[row].astype(jnp.float32)).astype(out.dtype)


VMEM = pl.BlockSpec(memory_space=pltpu.VMEM)
HBM = pl.BlockSpec(memory_space=pltpu.HBM)
ANY = pl.BlockSpec(memory_space=pl.ANY)


def held(x, space):
    return pltpu.with_memory_space_constraint(x, space)


def cost(e_shape, rows):
    macs = math.prod(e_shape) * rows
    return pl.CostEstimate(flops=2 * macs, bytes_accessed=BLOCK, transcendentals=0)


def run_first(place, offsets, assign, extrap, fronts, scale):
    nblk, band = extrap.shape[1:3]
    nfield, freqs, slots, points = fronts.shape
    rows = nfield * slots
    parts = math.gcd(PARTS, nblk)
    return pl.pallas_call(
        functools.partial(first_kernel, scale),
        out_shape=(
            pltpu.VMEM((nblk, rows, BLOCK), jnp.bfloat16),
            pltpu.VMEM((slots, nblk, BLOCK), jnp.float32),
            pltpu.VMEM((band + slots + 1, 8, BLOCK), jnp.int32),
            pltpu.VMEM(extrap.shape, extrap.dtype),
        ),
        in_specs=[VMEM, HBM, HBM, HBM, HBM],
        out_specs=(VMEM,) * 4,
        scratch_shapes=[
            pltpu.VMEM((nblk + 2 * (band // 2), rows, BLOCK), jnp.bfloat16),
            pltpu.SMEM(offsets.shape, jnp.int32),
            pltpu.SMEM(assign.shape, jnp.int32),
            pltpu.VMEM((nfield, slots, points), fronts.dtype),
            pltpu.SemaphoreType.DMA((parts,)),
            pltpu.SemaphoreType.DMA((3,)),
        ],
        compiler_params=pltpu.CompilerParams(vmem_limit_bytes=4 * 2**20),
        cost_estimate=cost(extrap.shape[1:], rows),
        name="first",
    )(held(place, pltpu.VMEM), *[held(x, pltpu.HBM) for x in (offsets, assign, extrap, fronts)])


def run_next(f, code, e, extrap, fronts, token, scale):
    nblk, band = e.shape[1:3]
    nfield, freqs, slots, points = fronts.shape
    rows = nfield * slots
    parts = math.gcd(PARTS, nblk)
    return pl.pallas_call(
        functools.partial(next_kernel, scale, f),
        out_shape=(
            pltpu.VMEM((nblk, rows, BLOCK), jnp.bfloat16),
            pltpu.VMEM((slots, nblk, BLOCK), jnp.float32),
            pltpu.VMEM(e.shape, e.dtype),
        ),
        in_specs=[VMEM, VMEM, HBM, HBM, ANY],
        out_specs=(VMEM,) * 3,
        scratch_shapes=[
            pltpu.VMEM((nblk + 2 * (band // 2), rows, BLOCK), jnp.bfloat16),
            pltpu.VMEM((nfield, slots, points), fronts.dtype),
            pltpu.SemaphoreType.DMA((parts,)),
            pltpu.SemaphoreType.DMA((1,)),
        ],
        input_output_aliases={1: 2},
        compiler_params=pltpu.CompilerParams(vmem_limit_bytes=4 * 2**20),
        cost_estimate=cost(e.shape[1:], rows),
        name="next",
    )(held(code, pltpu.VMEM), held(e, pltpu.VMEM), held(extrap, pltpu.HBM), held(fronts, pltpu.HBM), token)


def run_step(f, code, e, w, scale):
    nblk, band = e.shape[1:3]
    rows = w.shape[1]
    return pl.pallas_call(
        functools.partial(step_kernel, scale, f),
        out_shape=(
            pltpu.VMEM((nblk, rows, BLOCK), jnp.bfloat16),
            pltpu.VMEM((rows // 4, nblk, BLOCK), jnp.float32),
        ),
        in_specs=[VMEM, VMEM, VMEM],
        out_specs=(VMEM, VMEM),
        scratch_shapes=[pltpu.VMEM((nblk + 2 * (band // 2), rows, BLOCK), jnp.bfloat16)],
        compiler_params=pltpu.CompilerParams(vmem_limit_bytes=4 * 2**20),
        cost_estimate=cost(e.shape[1:], rows),
        name="step",
    )(*[held(x, pltpu.VMEM) for x in (code, e, w)])


def fold_owners(code, parts, rounds, owners):
    size = lax.axis_size("depth")
    rows, nblk, lanes = parts[0].shape
    left = owners // 2
    half = (left, rounds, nblk, lanes)
    small = pl.CostEstimate(flops=BLOCK, bytes_accessed=BLOCK, transcendentals=0)
    keep, send = pl.pallas_call(
        functools.partial(pair_kernel, len(parts) // rounds),
        out_shape=(pltpu.VMEM(half, jnp.float32), pltpu.VMEM(half, jnp.bfloat16)),
        in_specs=[VMEM] * (1 + len(parts)),
        out_specs=(VMEM, VMEM),
        compiler_params=pltpu.CompilerParams(vmem_limit_bytes=4 * 2**20),
        cost_estimate=small,
        name="pair",
    )(*[held(x, pltpu.VMEM) for x in (code, *parts)])
    came = lax.ppermute(send, "depth", [(i, i ^ 1) for i in range(size)])
    own, *others = pl.pallas_call(
        spread_kernel,
        out_shape=tuple(
            pltpu.VMEM(half[1:], jnp.bfloat16 if mask else jnp.float32) for mask in range(left)
        ),
        in_specs=[VMEM] * 3,
        out_specs=(VMEM,) * left,
        compiler_params=pltpu.CompilerParams(vmem_limit_bytes=4 * 2**20),
        cost_estimate=small,
        name="spread",
    )(*[held(x, pltpu.VMEM) for x in (code, keep, came)])
    for mask in ORDER:
        other = lax.ppermute(others[mask - 1], "depth", [(i, i ^ (2 * mask)) for i in range(size)])
        own = own + other.astype(jnp.float32)
    return own


def on_device(fronts, extrap, offsets, assign):
    sections = offsets.shape[0]
    size = lax.axis_size("depth")
    owners = size // sections
    index = lax.axis_index("depth")
    which = lax.broadcasted_iota(jnp.int32, (2, 8, BLOCK), 0)
    place = jnp.where(which == 0, lax.div(index, owners), lax.rem(index, owners)).astype(jnp.int32)
    nfield, freqs, slots, points = fronts.shape
    nblk = extrap.shape[1]
    scale = 1.0 / math.sqrt(2.0 * owners * freqs)
    onward = [(i, (i + owners) % size) for i in range(size)]
    waves, parts = [None] * freqs, []
    for r in range(HANDOVERS):
        for f in range(freqs):
            if r == 0 and f == 0:
                adv, img, code, e = run_first(place, offsets, assign, extrap, fronts, scale)
                token = lax.ppermute(img[:1], "depth", [(i, i ^ 1) for i in range(size)])
            elif r == 0:
                adv, img, e = run_next(f, code, e, extrap, fronts, token, scale)
            else:
                adv, img = run_step(f, code, e, waves[f], scale)
            parts.append(img)
            waves[f] = lax.ppermute(adv, "depth", onward) if r + 1 < HANDOVERS else adv
    images = fold_owners(code, parts, HANDOVERS, owners).reshape(HANDOVERS, 1, points)
    last = jnp.stack(waves).reshape(freqs, nblk, nfield, slots, BLOCK)
    last = last.transpose(2, 0, 3, 1, 4).reshape(fronts.shape)
    return images, last


def solution(mesh):
    placed = (
        P(None, ("groups", "depth"), None, None),
        P("depth", None, None, None, None, None),
        P(),
        P(),
    )
    return jax.shard_map(
        on_device,
        mesh=mesh,
        in_specs=placed,
        out_specs=(P(None, ("groups", "depth"), None), P(None, ("groups", "depth"), None, None)),
        check_vma=False,
    )
```
